256 devices in a mesh: prefix: 32 (over x, z), kvhead: 8 (over y, core).
Axes of the slice: x: 4, y: 4, z: 8, core: 2. Of those that a mesh axis runs over, the one named last changes fastest.
Arguments:
- queries: bfloat16 [256, 8192], P('prefix', 'kvhead')
- prefix_keys: bfloat16 [262144, 1024], P('prefix', 'kvhead')
- prefix_values: bfloat16 [262144, 1024], P('prefix', 'kvhead'), may hold values from -6 to 6
- suffix_keys: bfloat16 [256, 1024, 1024], P('prefix', None, 'kvhead'), may hold values from -12 to 12
- suffix_values: bfloat16 [256, 1024, 1024], P('prefix', None, 'kvhead'), may hold values from -6 to 6
- suffix_lengths: int32 [256], replicated, may hold values from 1 to 1024, 131072 in all
- slot_request: int32 [256], P('prefix'), may hold values from 0 to 255, each once
- out_weight: bfloat16 [8192, 8192], P('kvhead', 'prefix'), may hold values from -0.0625 to 0.0625
Outputs:
- mixed: bfloat16 [256, 8192], P('kvhead', 'prefix')
The draws below stay inside these ranges and needn't reach their ends.
Inputs may be any that keep to these rules, and one draw needn't show every extreme that they name: `suffix_lengths`: at least one continuation (in practice many) has all 1024 positions live; the others have uneven lengths. `slot_request`: each continuation sits in exactly one slot.
All inputs are finite; a program needn't handle non-finite values.
Results may differ from the reference program's by a relative error of at most 0.0065.
Values may be sent and summed in bfloat16 or wider, within the bound.
No kernel may reach another device: no remote copies, remote signals or barrier semaphores. Data moves between devices by JAX's collectives and lax.ppermute only.
A program may use at most 64 MiB of HBM per device.

```python
import math
import jax
import jax.numpy as jnp
import numpy as np
from jax import lax

D = 8192
Q_HEADS = 64
KV_HEADS = 8
HEAD_DIM = 128
GROUP = 8
BATCH = 256
SEG = 8192
PREFIX = 262144
S_MAX = 1024
N_PREFIX = 32


def shared_rows(key, positions):
    base = jax.random.fold_in(key, 77)

    def one_row(pos):
        return jax.random.normal(jax.random.fold_in(base, pos), (KV_HEADS * HEAD_DIM,), jnp.float32)
    return jax.vmap(one_row)(positions)


def draw_prefix_keys(key, part):
    return shared_rows(key, jnp.arange(PREFIX)).astype(jnp.bfloat16)


def draw_queries(key, part):
    key = jax.random.fold_in(key, 5)
    base = 1.5 * jax.random.normal(key, (BATCH, Q_HEADS * HEAD_DIM), jnp.float32)
    return base.astype(jnp.bfloat16)


def block_scale(key, dims, shards, low, top_value):
    gain = 1.0
    for position, parts in shards:
        steps = jax.random.uniform(jax.random.fold_in(jax.random.fold_in(key, 6), position), (parts,), jnp.float32, low / len(shards), top_value / len(shards))
        gain = gain * jnp.repeat(jnp.exp(steps), dims[position] // parts).reshape((-1,) + (1,) * (len(dims) - 1 - position))
    return gain


def profile(count, total, limit, slope):
    loads = [(1 << 20) // math.isqrt(grade ** slope) + 1 for grade in range(2, count + 1)]
    surplus, holding = total - limit - (count - 1), [1] * (count - 1)
    while surplus > 0:
        movable = [i for i in range(count - 1) if holding[i] < limit]
        pool, remaining = sum([loads[i] for i in movable]), surplus
        for i in movable:
            addition = min(limit - holding[i], max(1, remaining * loads[i] // pool), surplus)
            holding[i] = holding[i] + addition
            surplus = surplus - addition
    return np.array([limit] + holding)


def ragged_sizes(stream_key, amount, total, limit, slope):
    if amount == 2:
        one = jax.random.randint(stream_key, (), max(1, total - limit), min(limit, total - 1) + 1)
        return jnp.stack([one, total - one])
    sizes = jnp.asarray(profile(amount, total, limit, slope), jnp.int32)
    pairs = (amount - 1) // 2
    giver, taker = sizes[1:1 + 2 * pairs:2], sizes[2:2 + 2 * pairs:2]
    margin = jnp.minimum(giver - 1, limit - taker)
    passed = jax.random.randint(jax.random.fold_in(stream_key, 1), (pairs,), 0, 1 << 20) % (margin + 1)
    sizes = sizes.at[1:1 + 2 * pairs:2].set(giver - passed).at[2:2 + 2 * pairs:2].set(taker + passed)
    return sizes[jax.random.permutation(jax.random.fold_in(stream_key, 2), amount)]


def centred(rng, extent, spread, most, cuts=(), kind=jnp.bfloat16):
    values = jax.random.normal(rng, extent, jnp.float32) * spread
    if len(cuts) > 0:
        values = block_scale(rng, extent, cuts, -0.22, 0.18) * values
    return jnp.clip(values, min=-most, max=most).astype(kind)


def setup_inputs(seed: int = 0) -> dict:
    arg_keys = jax.random.split(jax.random.key(seed), 9)
    queries = draw_queries(jax.random.fold_in(arg_keys[8], 71), 0)
    prefix_keys = draw_prefix_keys(jax.random.fold_in(arg_keys[8], 71), 0)
    prefix_values = centred(arg_keys[2], (PREFIX, KV_HEADS * HEAD_DIM), 1.0, 6.0, ((0, 32), (1, 8)))
    suffix_keys = centred(arg_keys[3], (BATCH, S_MAX, KV_HEADS * HEAD_DIM), 2.0, 12.0, ((0, 32), (2, 8)))
    suffix_values = centred(arg_keys[4], (BATCH, S_MAX, KV_HEADS * HEAD_DIM), 1.0, 6.0, ((0, 32), (2, 8)))
    suffix_lengths = ragged_sizes(arg_keys[5], BATCH, BATCH * S_MAX // 2, S_MAX, 2).astype(jnp.int32)
    slot_request = jax.random.permutation(arg_keys[6], BATCH).astype(jnp.int32)
    out_weight = centred(arg_keys[7], (Q_HEADS * HEAD_DIM, D), (Q_HEADS * HEAD_DIM) ** -0.5, 0.0625, ((0, 8), (1, 32)))
    return dict(queries=queries, prefix_keys=prefix_keys, prefix_values=prefix_values, suffix_keys=suffix_keys, suffix_values=suffix_values, suffix_lengths=suffix_lengths, slot_request=slot_request, out_weight=out_weight)


def reference(queries, prefix_keys, prefix_values, suffix_keys, suffix_values, suffix_lengths, slot_request, out_weight):
    score_scale = HEAD_DIM ** -0.5
    lens = suffix_lengths[slot_request]
    live = jnp.arange(S_MAX)[None, :] < lens[:, None]
    q_all = jnp.moveaxis(queries.reshape(BATCH, KV_HEADS, GROUP, HEAD_DIM), 1, 0)
    pk = jnp.moveaxis(prefix_keys.reshape(PREFIX, KV_HEADS, HEAD_DIM), 1, 0)
    pv = jnp.moveaxis(prefix_values.reshape(PREFIX, KV_HEADS, HEAD_DIM), 1, 0)
    sk = jnp.moveaxis(suffix_keys.reshape(BATCH, S_MAX, KV_HEADS, HEAD_DIM), 2, 0)
    sv = jnp.moveaxis(suffix_values.reshape(BATCH, S_MAX, KV_HEADS, HEAD_DIM), 2, 0)

    def head_work(items):
        qg, kg, vg, skg, svg = items
        rows = qg.reshape(BATCH * GROUP, HEAD_DIM)

        def segment(kv):
            keys, values = kv
            scores = jnp.dot(rows, keys.T, preferred_element_type=jnp.float32) * score_scale
            peak = jnp.max(scores, axis=1)
            probs = jnp.exp(scores - peak[:, None]).astype(jnp.bfloat16)
            total = jnp.sum(probs.astype(jnp.float32), axis=1)
            numer = jnp.dot(probs, values, preferred_element_type=jnp.float32)
            ctx = (numer / total[:, None]).astype(jnp.bfloat16)
            return peak, total, ctx

        seg_max, seg_total, seg_ctx = lax.map(segment, (kg.reshape(N_PREFIX, SEG, HEAD_DIM), vg.reshape(N_PREFIX, SEG, HEAD_DIM)))
        seg_max = seg_max.reshape(N_PREFIX, BATCH, GROUP)
        seg_total = seg_total.reshape(N_PREFIX, BATCH, GROUP)
        seg_ctx = seg_ctx.reshape(N_PREFIX, BATCH, GROUP, HEAD_DIM).astype(jnp.float32)
        suf = jnp.einsum("bhe,bse->bhs", qg.astype(jnp.float32), skg.astype(jnp.float32)) * score_scale
        suf = jnp.where(live[:, None, :], suf, jnp.float32(-1e30))
        suf_max = jnp.max(suf, axis=2)
        suf_prob = jnp.where(live[:, None, :], jnp.exp(suf - suf_max[..., None]), jnp.float32(0.0)).astype(jnp.bfloat16)
        suf_total = jnp.sum(suf_prob.astype(jnp.float32), axis=2)
        suf_num = jnp.einsum("bhs,bse->bhe", suf_prob.astype(jnp.float32), svg.astype(jnp.float32))
        top = jnp.maximum(jnp.max(seg_max, axis=0), suf_max)
        weights = jnp.exp(seg_max - top[None]) * seg_total
        own = jnp.exp(suf_max - top)
        total = jnp.sum(weights, axis=0) + own * suf_total
        numer = jnp.sum(weights[..., None] * seg_ctx, axis=0) + own[..., None] * suf_num
        return (numer / total[..., None]).astype(jnp.bfloat16)

    context = lax.map(head_work, (q_all, pk, pv, sk, sv))
    context = jnp.moveaxis(context, 0, 1).reshape(BATCH, Q_HEADS * HEAD_DIM)
    return jnp.dot(context, out_weight, preferred_element_type=jnp.float32).astype(jnp.bfloat16)
```

```python
import functools
import math

import jax
import jax.numpy as jnp
from jax import lax
from jax.experimental import pallas as pl
from jax.experimental.pallas import tpu as pltpu
from jax.sharding import Mesh
from jax.sharding import PartitionSpec as P

HEAD_DIM = 128
GROUP = 8
WIDTH = GROUP * HEAD_DIM
PACKED = WIDTH + HEAD_DIM
SCALE2 = HEAD_DIM ** (-0.5) * math.log2(math.e)
CONTRACT_LAST = (((1,), (1,)), ((), ()))
VMEM_BYTES = 56 << 20


def split3(x):
    high = x.astype(jnp.bfloat16).astype(jnp.float32)
    rest = x - high
    mid = rest.astype(jnp.bfloat16).astype(jnp.float32)
    return high, mid, rest - mid


def store_scaled_rows(q_ref, rows_ref, slots):
    for g in range(GROUP):
        q = q_ref[:, g * HEAD_DIM : (g + 1) * HEAD_DIM].astype(jnp.float32) * SCALE2
        high = q.astype(jnp.bfloat16)
        low = (q - high.astype(jnp.float32)).astype(jnp.bfloat16)
        rows_ref[g * slots : (g + 1) * slots, :HEAD_DIM] = high
        rows_ref[g * slots : (g + 1) * slots, HEAD_DIM:] = low


def prefix_kernel(
    q_ref, k_hbm, v_hbm, out_ref, rows, keys, values, acc, peak, sems, *, slots, step, block
):
    count = k_hbm.shape[0] // step
    copies = []
    for j in range(count):
        part = pl.ds(j * step, step)
        copies.append(
            (
                pltpu.make_async_copy(k_hbm.at[part], keys.at[part], sems.at[0, j]),
                pltpu.make_async_copy(v_hbm.at[part], values.at[part], sems.at[1, j]),
            )
        )
    for pair in copies:
        for copy in pair:
            copy.start()
    store_scaled_rows(q_ref, rows, slots)
    total_rows = GROUP * slots

    def operands(part):
        k = keys[part, :]
        v = values[part, :]
        return (
            jnp.concatenate([k, k], axis=1),
            jnp.concatenate([v, jnp.ones_like(v)], axis=1),
        )

    for j in range(count):
        for copy in copies[j]:
            copy.wait()
        k2, v1 = operands(pl.ds(j * step, step))
        for r in range(0, total_rows, block):
            scores = lax.dot_general(
                rows[r : r + block, :], k2, CONTRACT_LAST, preferred_element_type=jnp.float32
            )
            probs = jnp.exp2(scores).astype(jnp.bfloat16)
            part = jnp.dot(probs, v1, preferred_element_type=jnp.float32)
            if j == 0:
                acc[r : r + block, :] = part
            else:
                acc[r : r + block, :] += part
    peak[...] = jnp.zeros_like(peak)
    sums = acc[:, HEAD_DIM:]
    fine = (sums >= 1e-25) & (sums <= 1e30)
    bad = jnp.max(jnp.where(fine, 0.0, 1.0))

    @pl.when(bad > 0.0)
    def _():
        peak[...] = jnp.full_like(peak, -1e38)
        acc[...] = jnp.zeros_like(acc)
        small = 512

        def body(i, carry):
            k2, v1 = operands(pl.ds(pl.multiple_of(i * small, small), small))

            def rows_body(r, inner):
                here = pl.ds(pl.multiple_of(r * block, block), block)
                scores = lax.dot_general(
                    rows[here, :], k2, CONTRACT_LAST, preferred_element_type=jnp.float32
                )
                old = peak[here, :]
                new = jnp.maximum(old, jnp.max(scores, axis=1, keepdims=True))
                probs = jnp.exp2(scores - new[:, :1]).astype(jnp.bfloat16)
                decay = jnp.exp2(old[:, :1] - new[:, :1])
                acc[here, :] = acc[here, :] * decay + jnp.dot(
                    probs, v1, preferred_element_type=jnp.float32
                )
                peak[here, :] = new
                return inner

            return lax.fori_loop(0, total_rows // block, rows_body, carry)

        lax.fori_loop(0, k_hbm.shape[0] // small, body, 0)

    lane = lax.broadcasted_iota(jnp.int32, (slots, HEAD_DIM), 1)
    stats = jnp.zeros((slots, HEAD_DIM), jnp.float32)
    for g in range(GROUP):
        here = slice(g * slots, (g + 1) * slots)
        sums = acc[here, HEAD_DIM:]
        out_ref[:, g * HEAD_DIM : (g + 1) * HEAD_DIM] = (
            acc[here, :HEAD_DIM] / sums
        ).astype(jnp.bfloat16)
        for i, piece in enumerate(split3(peak[here, :] + jnp.log2(sums))):
            stats = jnp.where(lane == i * GROUP + g, piece, stats)
    out_ref[:, WIDTH:] = stats.astype(jnp.bfloat16)


def prefix_part(queries, keys, values, step=2048, block=256):
    slots = queries.shape[0]
    length = keys.shape[0]
    rows = GROUP * slots
    return pl.pallas_call(
        functools.partial(prefix_kernel, slots=slots, step=step, block=block),
        in_specs=[
            pl.BlockSpec(memory_space=pltpu.VMEM),
            pl.BlockSpec(memory_space=pl.ANY),
            pl.BlockSpec(memory_space=pl.ANY),
        ],
        out_specs=pl.BlockSpec(memory_space=pltpu.VMEM),
        out_shape=jax.ShapeDtypeStruct((slots, PACKED), jnp.bfloat16),
        scratch_shapes=[
            pltpu.VMEM((rows, 2 * HEAD_DIM), jnp.bfloat16),
            pltpu.VMEM((length, HEAD_DIM), jnp.bfloat16),
            pltpu.VMEM((length, HEAD_DIM), jnp.bfloat16),
            pltpu.VMEM((rows, 2 * HEAD_DIM), jnp.float32),
            pltpu.VMEM((rows, HEAD_DIM), jnp.float32),
            pltpu.SemaphoreType.DMA((2, length // step)),
        ],
        compiler_params=pltpu.CompilerParams(vmem_limit_bytes=VMEM_BYTES),
        name="prefix_part",
    )(queries, keys, values)


def suffix_kernel(
    request_ref, lengths_ref, q_ref, k_hbm, v_hbm, ctx_ref, lse_ref, keys, values, sems
):
    slots, span = k_hbm.shape[0], k_hbm.shape[1]
    rows = GROUP * slots
    key_copies = [pltpu.make_async_copy(k_hbm.at[b], keys.at[b], sems.at[0, b]) for b in range(slots)]
    value_copies = [
        pltpu.make_async_copy(v_hbm.at[b], values.at[b], sems.at[1, b]) for b in range(slots)
    ]
    for copy in key_copies + value_copies:
        copy.start()
    q = jnp.concatenate(
        [q_ref[:, g * HEAD_DIM : (g + 1) * HEAD_DIM].astype(jnp.float32) for g in range(GROUP)],
        axis=0,
    ).astype(jnp.bfloat16)
    slot = lax.rem(lax.broadcasted_iota(jnp.int32, (rows, span), 0), slots)
    limit = jnp.zeros((rows, span), jnp.int32)
    for b in range(slots):
        limit = jnp.where(slot == b, lengths_ref[request_ref[b]], limit)
    live = lax.broadcasted_iota(jnp.int32, (rows, span), 1) < limit
    scores = jnp.zeros((rows, span), jnp.float32)
    for b in range(slots):
        key_copies[b].wait()
        mine = lax.dot_general(q, keys[b], CONTRACT_LAST, preferred_element_type=jnp.float32)
        scores = jnp.where(slot == b, mine, scores)
    scores = jnp.where(live, scores * SCALE2, -1e30)
    top = jnp.max(scores, axis=1, keepdims=True)
    probs = jnp.where(live, jnp.exp2(scores - top), 0.0).astype(jnp.bfloat16).astype(jnp.float32)
    total = jnp.sum(probs, axis=1, keepdims=True)
    numer = jnp.zeros((rows, HEAD_DIM), jnp.float32)
    for b in range(slots):
        value_copies[b].wait()
        mine = jnp.where(slot == b, probs, 0.0).astype(jnp.bfloat16)
        numer += jnp.dot(mine, values[b], preferred_element_type=jnp.float32)
    ctx = numer / total
    lse = jnp.broadcast_to(top + jnp.log2(total), (rows, HEAD_DIM))
    for g in range(GROUP):
        here = slice(g * slots, (g + 1) * slots)
        ctx_ref[:, g * HEAD_DIM : (g + 1) * HEAD_DIM] = ctx[here]
        lse_ref[:, g * HEAD_DIM : (g + 1) * HEAD_DIM] = lse[here]


def suffix_part(queries, keys, values, lengths, request):
    slots, span, _ = keys.shape
    vmem = pl.BlockSpec(memory_space=pltpu.VMEM)
    smem = pl.BlockSpec(memory_space=pltpu.SMEM)
    anywhere = pl.BlockSpec(memory_space=pl.ANY)
    return pl.pallas_call(
        suffix_kernel,
        in_specs=[smem, smem, vmem, anywhere, anywhere],
        out_specs=[vmem, vmem],
        out_shape=[jax.ShapeDtypeStruct((slots, WIDTH), jnp.float32)] * 2,
        scratch_shapes=[
            pltpu.VMEM((slots, span, HEAD_DIM), jnp.bfloat16),
            pltpu.VMEM((slots, span, HEAD_DIM), jnp.bfloat16),
            pltpu.SemaphoreType.DMA((2, slots)),
        ],
        compiler_params=pltpu.CompilerParams(vmem_limit_bytes=VMEM_BYTES),
        name="suffix_part",
    )(request, lengths, queries, keys, values)


def spread_lse(stats):
    source = lax.broadcasted_iota(jnp.int32, (HEAD_DIM, WIDTH), 0)
    head = lax.broadcasted_iota(jnp.int32, (HEAD_DIM, WIDTH), 1) // HEAD_DIM
    chosen = (lax.rem(source, GROUP) == head) & (source < 3 * GROUP)
    chosen = jnp.where(chosen, 1.0, 0.0).astype(jnp.bfloat16)
    return jnp.dot(stats, chosen, preferred_element_type=jnp.float32)


def merge_kernel(parts_ref, ctx_ref, lse_ref, out_ref, *, sources):
    slots = ctx_ref.shape[0]
    copies = out_ref.shape[0] // slots
    lse = spread_lse(parts_ref[:, WIDTH:])
    lse = [lse[i * slots : (i + 1) * slots] for i in range(sources)]
    top = functools.reduce(jnp.maximum, lse, lse_ref[...])
    weight = jnp.exp2(lse_ref[...] - top)
    total, numer = weight, weight * ctx_ref[...]
    parts = parts_ref[:, :WIDTH].astype(jnp.float32)
    for i in range(sources):
        weight = jnp.exp2(lse[i] - top)
        total += weight
        numer += weight * parts[i * slots : (i + 1) * slots]
    context = numer / total
    out_ref[...] = jnp.concatenate([context] * copies, axis=0).astype(jnp.bfloat16)


def merge(parts, ctx, lse, copies):
    slots = ctx.shape[0]
    return pl.pallas_call(
        functools.partial(merge_kernel, sources=parts.shape[0] // slots),
        out_shape=jax.ShapeDtypeStruct((copies * slots, WIDTH), jnp.bfloat16),
        compiler_params=pltpu.CompilerParams(vmem_limit_bytes=VMEM_BYTES),
        name="merge",
    )(parts, ctx, lse)


def on_device(
    queries,
    prefix_keys,
    prefix_values,
    suffix_keys,
    suffix_values,
    suffix_lengths,
    slot_request,
    out_weight,
):
    owners = lax.axis_size("prefix")
    swap = functools.partial(lax.all_to_all, axis_name="prefix", split_axis=0, concat_axis=0, tiled=True)
    everyone = swap(jnp.tile(queries, (owners, 1)))
    suffix_ctx, suffix_lse = suffix_part(
        queries, suffix_keys, suffix_values, suffix_lengths, slot_request
    )
    parts = swap(prefix_part(everyone, prefix_keys, prefix_values))
    context = swap(merge(parts, suffix_ctx, suffix_lse, owners))
    partial_out = jnp.dot(context, out_weight, preferred_element_type=jnp.float32)
    heads = lax.axis_size("kvhead")
    batch = partial_out.shape[0]
    pieces = lax.all_to_all(
        partial_out.astype(jnp.bfloat16), "kvhead", split_axis=0, concat_axis=0, tiled=True
    )
    pieces = pieces.reshape(heads, batch // heads, -1).astype(jnp.float32)
    return jnp.sum(pieces, axis=0).astype(jnp.bfloat16)


def solution(mesh):
    placed = (
        P("prefix", "kvhead"),
        P("prefix", "kvhead"),
        P("prefix", "kvhead"),
        P("prefix", None, "kvhead"),
        P("prefix", None, "kvhead"),
        P(),
        P("prefix"),
        P("kvhead", "prefix"),
    )
    return jax.shard_map(
        on_device, mesh=mesh, in_specs=placed, out_specs=P("kvhead", "prefix"), check_vma=False
    )
```

```python
import functools
import math

import jax
import jax.numpy as jnp
from jax import lax
from jax.experimental import pallas as pl
from jax.experimental.pallas import tpu as pltpu
from jax.sharding import Mesh
from jax.sharding import PartitionSpec as P

HEAD_DIM = 128
GROUP = 8
WIDTH = GROUP * HEAD_DIM
PACKED = WIDTH + HEAD_DIM
SCALE2 = HEAD_DIM ** (-0.5) * math.log2(math.e)
CONTRACT_LAST = (((1,), (1,)), ((), ()))
PREFIX_VMEM = 24 << 20
SUFFIX_VMEM = 12 << 20
MERGE_VMEM = 12 << 20


def split3(x):
    high = x.astype(jnp.bfloat16).astype(jnp.float32)
    rest = x - high
    mid = rest.astype(jnp.bfloat16).astype(jnp.float32)
    return high, mid, rest - mid


def operands(k, v):
    return jnp.concatenate([k, k], axis=1), jnp.concatenate([v, jnp.ones_like(v)], axis=1)


def put_queries(rows, base, blocks):
    q = jnp.concatenate([block.astype(jnp.float32) for block in blocks], axis=0) * SCALE2
    slots = q.shape[0]
    for g in range(GROUP):
        here = slice(base + g * slots, base + (g + 1) * slots)
        mine = q[:, g * HEAD_DIM : (g + 1) * HEAD_DIM]
        high = mine.astype(jnp.bfloat16)
        rows[here, :HEAD_DIM] = high
        rows[here, HEAD_DIM:] = (mine - high.astype(jnp.float32)).astype(jnp.bfloat16)


def attend(rows, k_ref, v_ref, acc, peak, step, block):
    total_rows = rows.shape[0]
    length = k_ref.shape[0]
    for j in range(0, length, step):
        k2, v1 = operands(k_ref[j : j + step, :], v_ref[j : j + step, :])
        for r in range(0, total_rows, block):
            scores = lax.dot_general(
                rows[r : r + block, :], k2, CONTRACT_LAST, preferred_element_type=jnp.float32
            )
            probs = jnp.exp2(scores).astype(jnp.bfloat16)
            part = jnp.dot(probs, v1, preferred_element_type=jnp.float32)
            if j == 0:
                acc[r : r + block, :] = part
            else:
                acc[r : r + block, :] += part
    peak[...] = jnp.zeros_like(peak)
    sums = acc[:, HEAD_DIM:]
    fine = (sums >= 1e-25) & (sums <= 1e30)
    bad = jnp.max(jnp.where(fine, 0.0, 1.0))

    @pl.when(bad > 0.0)
    def _():
        peak[...] = jnp.full_like(peak, -1e38)
        acc[...] = jnp.zeros_like(acc)
        small, few = 512, 128

        def body(i, carry):
            part = pl.ds(pl.multiple_of(i * small, small), small)
            k2, v1 = operands(k_ref[part, :], v_ref[part, :])

            def rows_body(r, inner):
                here = pl.ds(pl.multiple_of(r * few, few), few)
                scores = lax.dot_general(
                    rows[here, :], k2, CONTRACT_LAST, preferred_element_type=jnp.float32
                )
                old = peak[here, :]
                new = jnp.maximum(old, jnp.max(scores, axis=1, keepdims=True))
                probs = jnp.exp2(scores - new[:, :1]).astype(jnp.bfloat16)
                decay = jnp.exp2(old[:, :1] - new[:, :1])
                acc[here, :] = acc[here, :] * decay + jnp.dot(
                    probs, v1, preferred_element_type=jnp.float32
                )
                peak[here, :] = new
                return inner

            return lax.fori_loop(0, total_rows // few, rows_body, carry)

        lax.fori_loop(0, length // small, body, 0)


def packed(acc, peak, base, slots):
    lane = lax.broadcasted_iota(jnp.int32, (slots, HEAD_DIM), 1)
    stats = jnp.zeros((slots, HEAD_DIM), jnp.float32)
    pieces = []
    for g in range(GROUP):
        here = slice(base + g * slots, base + (g + 1) * slots)
        sums = acc[here, HEAD_DIM:]
        pieces.append((acc[here, :HEAD_DIM] / sums).astype(jnp.bfloat16))
        for n, piece in enumerate(split3(peak[here, :] + jnp.log2(sums))):
            stats = jnp.where(lane == n * GROUP + g, piece, stats)
    return jnp.concatenate(pieces + [stats.astype(jnp.bfloat16)], axis=1)


def first_kernel(
    q_ref, k_ref, v_ref, suffix_ctx_ref, suffix_lse_ref, out_ref, rows, acc, peak, *, step, block
):
    classes = out_ref.shape[0]
    along, held, _ = q_ref.shape
    halves = along // classes
    order = [(c, h) for c in range(classes) for h in range(halves)]
    slots = along * held
    put_queries(rows, 0, [q_ref[h * classes + c] for c, h in order])
    attend(rows, k_ref, v_ref, acc, peak, step, block)
    here_z = lax.axis_index("z")
    place = (lax.rem(here_z, classes) * halves + here_z // classes) * held
    for g in range(GROUP):
        here = pl.ds(pl.multiple_of(g * slots + place, held), held)
        lanes = slice(g * HEAD_DIM, (g + 1) * HEAD_DIM)
        sums = acc[here, HEAD_DIM:]
        prefix_lse = peak[here, :] + jnp.log2(sums)
        suffix_lse = suffix_lse_ref[:, lanes]
        top = jnp.maximum(prefix_lse, suffix_lse)
        from_prefix = jnp.exp2(prefix_lse - top)
        from_suffix = jnp.exp2(suffix_lse - top)
        both = from_prefix + from_suffix
        acc[here, :HEAD_DIM] = (
            from_prefix * (acc[here, :HEAD_DIM] / sums) + from_suffix * suffix_ctx_ref[:, lanes]
        ) / both
        acc[here, HEAD_DIM:] = jnp.ones_like(sums)
        peak[here, :] = top + jnp.log2(both)
    out = packed(acc, peak, 0, slots)
    size = halves * held
    for c in range(classes):
        out_ref[c] = out[c * size : (c + 1) * size]


def class_kernel(*refs, turns, step, block):
    *q_refs, k_ref, v_ref, first_ref = refs[: -len(turns) - 3]
    out_refs = refs[-len(turns) - 3 : -3]
    rows, acc, peak = refs[-3:]
    across = first_ref.shape[0]
    along, held, _ = q_refs[0].shape
    halves = along // across
    size = halves * held
    slots = len(q_refs) * size
    here_x = lax.axis_index("x")
    kinds = [lax.rem(here_x + turn, across) for turn in turns]
    for i, kind in enumerate(kinds):
        put_queries(
            rows,
            i * GROUP * slots,
            [q_ref[h * across + kind] for q_ref in q_refs for h in range(halves)],
        )
    attend(rows, k_ref, v_ref, acc, peak, step, block)
    for i, kind in enumerate(kinds):
        out = packed(acc, peak, i * GROUP * slots, slots)
        for n in range(len(q_refs)):
            at = lax.rem(here_x + across - n - 1, across)
            there = pl.ds(pl.multiple_of(at * size, size), size)
            out_refs[i][there, :] = out[n * size : (n + 1) * size]
        there = pl.ds(pl.multiple_of(here_x * size, size), size)
        out_refs[i][there, :] = first_ref[kind]


def prefix_call(kernel, rows, length, operand_list, out_dims, name):
    vmem = pl.BlockSpec(memory_space=pltpu.VMEM)
    return pl.pallas_call(
        kernel,
        in_specs=[vmem] * len(operand_list),
        out_specs=[vmem] * len(out_dims),
        out_shape=[jax.ShapeDtypeStruct(dims, jnp.bfloat16) for dims in out_dims],
        scratch_shapes=[
            pltpu.VMEM((rows, 2 * HEAD_DIM), jnp.bfloat16),
            pltpu.VMEM((rows, 2 * HEAD_DIM), jnp.float32),
            pltpu.VMEM((rows, HEAD_DIM), jnp.float32),
        ],
        compiler_params=pltpu.CompilerParams(vmem_limit_bytes=PREFIX_VMEM),
        cost_estimate=pl.CostEstimate(
            flops=8 * rows * length * HEAD_DIM,
            bytes_accessed=4 * length * HEAD_DIM,
            transcendentals=rows * length,
        ),
        name=name,
    )(*operand_list)


def first_part(queries, keys, values, suffix_ctx, suffix_lse, classes):
    along, held, _ = queries.shape
    return prefix_call(
        functools.partial(first_kernel, step=4096, block=256),
        GROUP * along * held,
        keys.shape[0],
        (queries, keys, values, suffix_ctx, suffix_lse),
        [(classes, along * held // classes, PACKED)],
        "first_part",
    )[0]


def class_part(queries, keys, values, first, turns):
    classes, size, _ = first.shape
    rows = GROUP * len(queries) * size
    return prefix_call(
        functools.partial(class_kernel, turns=turns, step=4096, block=rows),
        rows * len(turns),
        keys.shape[0],
        (*queries, keys, values, first),
        [(classes * size, PACKED)] * len(turns),
        "class_part",
    )


def suffix_kernel(request_ref, lengths_ref, q_ref, keys, values, ctx_ref, lse_ref):
    slots, span = keys.shape[0], keys.shape[1]
    rows = GROUP * slots
    q = jnp.concatenate(
        [q_ref[:, g * HEAD_DIM : (g + 1) * HEAD_DIM].astype(jnp.float32) for g in range(GROUP)],
        axis=0,
    ).astype(jnp.bfloat16)
    slot = lax.rem(lax.broadcasted_iota(jnp.int32, (rows, span), 0), slots)
    limit = jnp.zeros((rows, span), jnp.int32)
    for b in range(slots):
        limit = jnp.where(slot == b, lengths_ref[request_ref[b]], limit)
    live = lax.broadcasted_iota(jnp.int32, (rows, span), 1) < limit
    scores = jnp.zeros((rows, span), jnp.float32)
    for b in range(slots):
        mine = lax.dot_general(q, keys[b], CONTRACT_LAST, preferred_element_type=jnp.float32)
        scores = jnp.where(slot == b, mine, scores)
    scores = jnp.where(live, scores * SCALE2, -1e30)
    top = jnp.max(scores, axis=1, keepdims=True)
    probs = jnp.where(live, jnp.exp2(scores - top), 0.0).astype(jnp.bfloat16).astype(jnp.float32)
    total = jnp.sum(probs, axis=1, keepdims=True)
    numer = jnp.zeros((rows, HEAD_DIM), jnp.float32)
    for b in range(slots):
        mine = jnp.where(slot == b, probs, 0.0).astype(jnp.bfloat16)
        numer += jnp.dot(mine, values[b], preferred_element_type=jnp.float32)
    ctx = numer / total
    lse = jnp.broadcast_to(top + jnp.log2(total), (rows, HEAD_DIM))
    for g in range(GROUP):
        here = slice(g * slots, (g + 1) * slots)
        ctx_ref[:, g * HEAD_DIM : (g + 1) * HEAD_DIM] = ctx[here]
        lse_ref[:, g * HEAD_DIM : (g + 1) * HEAD_DIM] = lse[here]


def suffix_part(queries, keys, values, lengths, request):
    slots = keys.shape[0]
    vmem = pl.BlockSpec(memory_space=pltpu.VMEM)
    smem = pl.BlockSpec(memory_space=pltpu.SMEM)
    return pl.pallas_call(
        suffix_kernel,
        in_specs=[smem, smem, vmem, vmem, vmem],
        out_specs=[vmem, vmem],
        out_shape=[jax.ShapeDtypeStruct((slots, WIDTH), jnp.float32)] * 2,
        compiler_params=pltpu.CompilerParams(vmem_limit_bytes=SUFFIX_VMEM),
        name="suffix_part",
    )(request, lengths, queries, keys, values)


def spread_lse(stats):
    source = lax.broadcasted_iota(jnp.int32, (HEAD_DIM, WIDTH), 0)
    head = lax.broadcasted_iota(jnp.int32, (HEAD_DIM, WIDTH), 1) // HEAD_DIM
    chosen = (lax.rem(source, GROUP) == head) & (source < 3 * GROUP)
    chosen = jnp.where(chosen, 1.0, 0.0).astype(jnp.bfloat16)
    return jnp.dot(stats, chosen, preferred_element_type=jnp.float32)


def weighted(parts, lse):
    top = functools.reduce(jnp.maximum, lse)
    total, numer = 0.0, 0.0
    for part, each in zip(parts, lse, strict=True):
        weight = jnp.exp2(each - top)
        total += weight
        numer += weight * part
    return numer / total, top + jnp.log2(total)


def pack_lse(lse):
    rows = lse.shape[0]
    lane = lax.broadcasted_iota(jnp.int32, (rows, HEAD_DIM), 1)
    stats = jnp.zeros((rows, HEAD_DIM), jnp.float32)
    for g in range(GROUP):
        for n, piece in enumerate(split3(lse[:, g * HEAD_DIM : (g + 1) * HEAD_DIM])):
            stats = jnp.where(lane == n * GROUP + g, piece, stats)
    return stats.astype(jnp.bfloat16)


def merge_x_kernel(*refs):
    *part_refs, out_ref = refs
    ctx, both = weighted(
        [part[:, :WIDTH].astype(jnp.float32) for part in part_refs],
        [spread_lse(part[:, WIDTH:]) for part in part_refs],
    )
    out_ref[:, :WIDTH] = ctx.astype(jnp.bfloat16)
    out_ref[:, WIDTH:] = pack_lse(both)


def merge_x(parts):
    return pl.pallas_call(
        merge_x_kernel,
        out_shape=jax.ShapeDtypeStruct(parts[0].shape, jnp.bfloat16),
        compiler_params=pltpu.CompilerParams(vmem_limit_bytes=MERGE_VMEM),
        name="merge_x",
    )(*parts)


def merge_z_kernel(parts_ref, out_ref, *, sources):
    slots = parts_ref.shape[0] // sources
    lse = spread_lse(parts_ref[:, WIDTH:])
    parts = parts_ref[:, :WIDTH].astype(jnp.float32)
    cut = [slice(i * slots, (i + 1) * slots) for i in range(sources)]
    context, _ = weighted([parts[c] for c in cut], [lse[c] for c in cut])
    out_ref[...] = jnp.concatenate([context] * (out_ref.shape[0] // slots), axis=0).astype(jnp.bfloat16)


def merge_z(parts, sources, copies):
    return pl.pallas_call(
        functools.partial(merge_z_kernel, sources=sources),
        out_shape=jax.ShapeDtypeStruct((parts.shape[0] // sources * copies, WIDTH), jnp.bfloat16),
        compiler_params=pltpu.CompilerParams(vmem_limit_bytes=MERGE_VMEM),
        name="merge_z",
    )(parts)


def project_kernel(context_ref, weight_ref, out_ref):
    blocks, size, _ = out_ref.shape
    product = jnp.dot(context_ref[...], weight_ref[...], preferred_element_type=jnp.float32)
    held = 8
    for b in range(blocks):
        mine = [
            product[(c * blocks + b) * held : (c * blocks + b + 1) * held]
            for c in range(size // held)
        ]
        out_ref[b] = jnp.concatenate(mine, axis=0).astype(jnp.bfloat16)


def project(context, weight, blocks):
    return pl.pallas_call(
        project_kernel,
        out_shape=jax.ShapeDtypeStruct(
            (blocks, context.shape[0] // blocks, weight.shape[1]), jnp.bfloat16
        ),
        compiler_params=pltpu.CompilerParams(vmem_limit_bytes=MERGE_VMEM),
        name="project",
    )(context, weight)


def swap(array, axes):
    return lax.all_to_all(array, axes, split_axis=0, concat_axis=0, tiled=True)


def on_device(
    queries,
    prefix_keys,
    prefix_values,
    suffix_keys,
    suffix_values,
    suffix_lengths,
    slot_request,
    out_weight,
):
    held = queries.shape[0]
    across, along, heads = lax.axis_size("x"), lax.axis_size("z"), lax.axis_size("kvhead")
    near = swap(jnp.tile(queries, (along, 1)), "z")
    near, own_queries = lax.optimization_barrier((near, queries))

    def to_other_x(array, turn):
        return lax.ppermute(array, "x", [(i, (i + turn) % across) for i in range(across)])

    turns = range(1, across)
    near = near.reshape(along, held, WIDTH)
    far = [to_other_x(near, turn) for turn in turns]
    suffix_ctx, suffix_lse = suffix_part(
        own_queries, suffix_keys, suffix_values, suffix_lengths, slot_request
    )
    first = first_part(near, prefix_keys, prefix_values, suffix_ctx, suffix_lse, across)
    first, *far = lax.optimization_barrier((first, *far))
    leaving = class_part(far, prefix_keys, prefix_values, first, tuple(turns))
    first, *leaving = lax.optimization_barrier((first, *leaving))
    arrived = [to_other_x(part, turn) for part, turn in zip(leaving, turns, strict=True)]
    staying = class_part(far, prefix_keys, prefix_values, first, (0,))
    partial = merge_x([*staying, *arrived])
    context = swap(merge_z(swap(partial, "z"), along, across * along), ("x", "z"))
    out = project(context, out_weight, heads)
    pieces = swap(out.reshape(-1, out.shape[2]), "kvhead")
    pieces = pieces.reshape(heads, across * held, -1).astype(jnp.float32)
    return jnp.sum(pieces, axis=0).astype(jnp.bfloat16)


def solution(mesh):
    x_chips = 4
    devices = mesh.devices
    split = Mesh(
        devices.reshape(x_chips, devices.shape[0] // x_chips, devices.shape[1]),
        ("x", "z", "kvhead"),
    )
    prefix = ("x", "z")
    placed = (
        P(prefix, "kvhead"),
        P(prefix, "kvhead"),
        P(prefix, "kvhead"),
        P(prefix, None, "kvhead"),
        P(prefix, None, "kvhead"),
        P(),
        P(prefix),
        P("kvhead", prefix),
    )
    return jax.shard_map(
        on_device, mesh=split, in_specs=placed, out_specs=P("kvhead", prefix), check_vma=False
    )
```

```python
import functools
import math

import jax
import jax.numpy as jnp
from jax import lax
from jax.experimental import pallas as pl
from jax.experimental.pallas import tpu as pltpu
from jax.sharding import Mesh
from jax.sharding import PartitionSpec as P

HEAD_DIM = 128
GROUP = 8
WIDTH = GROUP * HEAD_DIM
PACKED = WIDTH + HEAD_DIM
SCALE2 = HEAD_DIM ** (-0.5) * math.log2(math.e)
CONTRACT_LAST = (((1,), (1,)), ((), ()))
PREFIX_VMEM = 24 << 20
SUFFIX_VMEM = 12 << 20
MERGE_VMEM = 12 << 20


def split3(x):
    high = x.astype(jnp.bfloat16).astype(jnp.float32)
    rest = x - high
    mid = rest.astype(jnp.bfloat16).astype(jnp.float32)
    return high, mid, rest - mid


def operands(k, v):
    return jnp.concatenate([k, k], axis=1), jnp.concatenate([v, jnp.ones_like(v)], axis=1)


def put_queries(rows, base, blocks):
    q = jnp.concatenate([block.astype(jnp.float32) for block in blocks], axis=0) * SCALE2
    slots = q.shape[0]
    for g in range(GROUP):
        here = slice(base + g * slots, base + (g + 1) * slots)
        mine = q[:, g * HEAD_DIM : (g + 1) * HEAD_DIM]
        high = mine.astype(jnp.bfloat16)
        rows[here, :HEAD_DIM] = high
        rows[here, HEAD_DIM:] = (mine - high.astype(jnp.float32)).astype(jnp.bfloat16)


def attend(rows, k_ref, v_ref, acc, peak, step, block):
    total_rows = rows.shape[0]
    length = k_ref.shape[0]
    for j in range(0, length, step):
        k2, v1 = operands(k_ref[j : j + step, :], v_ref[j : j + step, :])
        for r in range(0, total_rows, block):
            scores = lax.dot_general(
                rows[r : r + block, :], k2, CONTRACT_LAST, preferred_element_type=jnp.float32
            )
            probs = jnp.exp2(scores).astype(jnp.bfloat16)
            part = jnp.dot(probs, v1, preferred_element_type=jnp.float32)
            if j == 0:
                acc[r : r + block, :] = part
            else:
                acc[r : r + block, :] += part
    peak[...] = jnp.zeros_like(peak)
    sums = acc[:, HEAD_DIM:]
    fine = (sums >= 1e-25) & (sums <= 1e30)
    bad = jnp.max(jnp.where(fine, 0.0, 1.0))

    @pl.when(bad > 0.0)
    def _():
        peak[...] = jnp.full_like(peak, -1e38)
        acc[...] = jnp.zeros_like(acc)
        small, few = 512, 128

        def body(i, carry):
            part = pl.ds(pl.multiple_of(i * small, small), small)
            k2, v1 = operands(k_ref[part, :], v_ref[part, :])

            def rows_body(r, inner):
                here = pl.ds(pl.multiple_of(r * few, few), few)
                scores = lax.dot_general(
                    rows[here, :], k2, CONTRACT_LAST, preferred_element_type=jnp.float32
                )
                old = peak[here, :]
                new = jnp.maximum(old, jnp.max(scores, axis=1, keepdims=True))
                probs = jnp.exp2(scores - new[:, :1]).astype(jnp.bfloat16)
                decay = jnp.exp2(old[:, :1] - new[:, :1])
                acc[here, :] = acc[here, :] * decay + jnp.dot(
                    probs, v1, preferred_element_type=jnp.float32
                )
                peak[here, :] = new
                return inner

            return lax.fori_loop(0, total_rows // few, rows_body, carry)

        lax.fori_loop(0, length // small, body, 0)


def packed(acc, peak, base, slots):
    lane = lax.broadcasted_iota(jnp.int32, (slots, HEAD_DIM), 1)
    stats = jnp.zeros((slots, HEAD_DIM), jnp.float32)
    pieces = []
    for g in range(GROUP):
        here = slice(base + g * slots, base + (g + 1) * slots)
        sums = acc[here, HEAD_DIM:]
        pieces.append((acc[here, :HEAD_DIM] / sums).astype(jnp.bfloat16))
        for n, piece in enumerate(split3(peak[here, :] + jnp.log2(sums))):
            stats = jnp.where(lane == n * GROUP + g, piece, stats)
    return jnp.concatenate(pieces + [stats.astype(jnp.bfloat16)], axis=1)


def first_kernel(q_ref, k_ref, v_ref, out_ref, rows, acc, peak, *, step, block):
    classes = out_ref.shape[0]
    along, held, _ = q_ref.shape
    halves = along // classes
    order = [(c, h) for c in range(classes) for h in range(halves)]
    slots = along * held
    put_queries(rows, 0, [q_ref[h * classes + c] for c, h in order])
    attend(rows, k_ref, v_ref, acc, peak, step, block)
    out = packed(acc, peak, 0, slots)
    size = halves * held
    for c in range(classes):
        out_ref[c] = out[c * size : (c + 1) * size]


def class_kernel(*refs, turns, step, block):
    *q_refs, k_ref, v_ref, first_ref = refs[: -len(turns) - 3]
    out_refs = refs[-len(turns) - 3 : -3]
    rows, acc, peak = refs[-3:]
    across = first_ref.shape[0]
    along, held, _ = q_refs[0].shape
    halves = along // across
    size = halves * held
    slots = len(q_refs) * size
    here_x = lax.axis_index("x")
    kinds = [lax.rem(here_x + turn, across) for turn in turns]
    for i, kind in enumerate(kinds):
        put_queries(
            rows,
            i * GROUP * slots,
            [q_ref[h * across + kind] for q_ref in q_refs for h in range(halves)],
        )
    attend(rows, k_ref, v_ref, acc, peak, step, block)
    for i, kind in enumerate(kinds):
        out = packed(acc, peak, i * GROUP * slots, slots)
        for n in range(len(q_refs)):
            at = lax.rem(here_x + across - n - 1, across)
            there = pl.ds(pl.multiple_of(at * size, size), size)
            out_refs[i][there, :] = out[n * size : (n + 1) * size]
        there = pl.ds(pl.multiple_of(here_x * size, size), size)
        out_refs[i][there, :] = first_ref[kind]


def prefix_call(kernel, rows, length, operand_list, out_dims, name):
    vmem = pl.BlockSpec(memory_space=pltpu.VMEM)
    return pl.pallas_call(
        kernel,
        in_specs=[vmem] * len(operand_list),
        out_specs=[vmem] * len(out_dims),
        out_shape=[jax.ShapeDtypeStruct(dims, jnp.bfloat16) for dims in out_dims],
        scratch_shapes=[
            pltpu.VMEM((rows, 2 * HEAD_DIM), jnp.bfloat16),
            pltpu.VMEM((rows, 2 * HEAD_DIM), jnp.float32),
            pltpu.VMEM((rows, HEAD_DIM), jnp.float32),
        ],
        compiler_params=pltpu.CompilerParams(vmem_limit_bytes=PREFIX_VMEM),
        cost_estimate=pl.CostEstimate(
            flops=8 * rows * length * HEAD_DIM,
            bytes_accessed=4 * length * HEAD_DIM,
            transcendentals=rows * length,
        ),
        name=name,
    )(*operand_list)


def first_part(queries, keys, values, classes):
    along, held, _ = queries.shape
    return prefix_call(
        functools.partial(first_kernel, step=4096, block=256),
        GROUP * along * held,
        keys.shape[0],
        (queries, keys, values),
        [(classes, along * held // classes, PACKED)],
        "first_part",
    )[0]


def class_part(queries, keys, values, first, turns):
    classes, size, _ = first.shape
    rows = GROUP * len(queries) * size
    return prefix_call(
        functools.partial(class_kernel, turns=turns, step=4096, block=rows),
        rows * len(turns),
        keys.shape[0],
        (*queries, keys, values, first),
        [(classes * size, PACKED)] * len(turns),
        "class_part",
    )


def suffix_kernel(request_ref, lengths_ref, q_ref, keys, values, first_ref, out_ref):
    slots, span = keys.shape[0], keys.shape[1]
    rows = GROUP * slots
    q = jnp.concatenate(
        [q_ref[:, g * HEAD_DIM : (g + 1) * HEAD_DIM].astype(jnp.float32) for g in range(GROUP)],
        axis=0,
    ).astype(jnp.bfloat16)
    slot = lax.rem(lax.broadcasted_iota(jnp.int32, (rows, span), 0), slots)
    limit = jnp.zeros((rows, span), jnp.int32)
    for b in range(slots):
        limit = jnp.where(slot == b, lengths_ref[request_ref[b]], limit)
    live = lax.broadcasted_iota(jnp.int32, (rows, span), 1) < limit
    scores = jnp.zeros((rows, span), jnp.float32)
    for b in range(slots):
        mine = lax.dot_general(q, keys[b], CONTRACT_LAST, preferred_element_type=jnp.float32)
        scores = jnp.where(slot == b, mine, scores)
    scores = jnp.where(live, scores * SCALE2, -1e30)
    top = jnp.max(scores, axis=1, keepdims=True)
    probs = jnp.where(live, jnp.exp2(scores - top), 0.0).astype(jnp.bfloat16).astype(jnp.float32)
    total = jnp.sum(probs, axis=1, keepdims=True)
    numer = jnp.zeros((rows, HEAD_DIM), jnp.float32)
    for b in range(slots):
        mine = jnp.where(slot == b, probs, 0.0).astype(jnp.bfloat16)
        numer += jnp.dot(mine, values[b], preferred_element_type=jnp.float32)
    ctx = numer / total
    lse = jnp.broadcast_to(top + jnp.log2(total), (rows, HEAD_DIM))
    classes, size, _ = first_ref.shape
    here_z = lax.axis_index("z")
    kind, half = lax.rem(here_z, classes), here_z // classes
    own = lax.broadcasted_iota(jnp.int32, (size, WIDTH), 0) // slots == half

    def across_lanes(array):
        array = jnp.concatenate([array[g * slots : (g + 1) * slots] for g in range(GROUP)], axis=1)
        return jnp.concatenate([array] * (size // slots), axis=0)

    prefix = first_ref[kind]
    prefix_ctx = prefix[:, :WIDTH].astype(jnp.float32)
    prefix_lse = spread_lse(prefix[:, WIDTH:])
    both_ctx, both_lse = weighted([prefix_ctx, across_lanes(ctx)], [prefix_lse, across_lanes(lse)])
    out_ref[...] = first_ref[...]
    out_ref[kind, :, :WIDTH] = jnp.where(own, both_ctx, prefix_ctx).astype(jnp.bfloat16)
    out_ref[kind, :, WIDTH:] = pack_lse(jnp.where(own, both_lse, prefix_lse))


def suffix_part(queries, keys, values, lengths, request, first):
    vmem = pl.BlockSpec(memory_space=pltpu.VMEM)
    smem = pl.BlockSpec(memory_space=pltpu.SMEM)
    return pl.pallas_call(
        suffix_kernel,
        in_specs=[smem, smem, vmem, vmem, vmem, vmem],
        out_specs=vmem,
        out_shape=jax.ShapeDtypeStruct(first.shape, jnp.bfloat16),
        compiler_params=pltpu.CompilerParams(vmem_limit_bytes=SUFFIX_VMEM),
        name="suffix_part",
    )(request, lengths, queries, keys, values, first)


def spread_lse(stats):
    source = lax.broadcasted_iota(jnp.int32, (HEAD_DIM, WIDTH), 0)
    head = lax.broadcasted_iota(jnp.int32, (HEAD_DIM, WIDTH), 1) // HEAD_DIM
    chosen = (lax.rem(source, GROUP) == head) & (source < 3 * GROUP)
    chosen = jnp.where(chosen, 1.0, 0.0).astype(jnp.bfloat16)
    return jnp.dot(stats, chosen, preferred_element_type=jnp.float32)


def weighted(parts, lse):
    top = functools.reduce(jnp.maximum, lse)
    total, numer = 0.0, 0.0
    for part, each in zip(parts, lse, strict=True):
        weight = jnp.exp2(each - top)
        total += weight
        numer += weight * part
    return numer / total, top + jnp.log2(total)


def pack_lse(lse):
    rows = lse.shape[0]
    lane = lax.broadcasted_iota(jnp.int32, (rows, HEAD_DIM), 1)
    stats = jnp.zeros((rows, HEAD_DIM), jnp.float32)
    for g in range(GROUP):
        for n, piece in enumerate(split3(lse[:, g * HEAD_DIM : (g + 1) * HEAD_DIM])):
            stats = jnp.where(lane == n * GROUP + g, piece, stats)
    return stats.astype(jnp.bfloat16)


def merge_x_kernel(*refs):
    *part_refs, out_ref = refs
    ctx, both = weighted(
        [part[:, :WIDTH].astype(jnp.float32) for part in part_refs],
        [spread_lse(part[:, WIDTH:]) for part in part_refs],
    )
    out_ref[:, :WIDTH] = ctx.astype(jnp.bfloat16)
    out_ref[:, WIDTH:] = pack_lse(both)


def merge_x(parts):
    return pl.pallas_call(
        merge_x_kernel,
        out_shape=jax.ShapeDtypeStruct(parts[0].shape, jnp.bfloat16),
        compiler_params=pltpu.CompilerParams(vmem_limit_bytes=MERGE_VMEM),
        name="merge_x",
    )(*parts)


def merge_z_kernel(parts_ref, out_ref, *, sources):
    slots = parts_ref.shape[0] // sources
    lse = spread_lse(parts_ref[:, WIDTH:])
    parts = parts_ref[:, :WIDTH].astype(jnp.float32)
    cut = [slice(i * slots, (i + 1) * slots) for i in range(sources)]
    context, _ = weighted([parts[c] for c in cut], [lse[c] for c in cut])
    out_ref[...] = jnp.concatenate([context] * (out_ref.shape[0] // slots), axis=0).astype(jnp.bfloat16)


def merge_z(parts, sources, copies):
    return pl.pallas_call(
        functools.partial(merge_z_kernel, sources=sources),
        out_shape=jax.ShapeDtypeStruct((parts.shape[0] // sources * copies, WIDTH), jnp.bfloat16),
        compiler_params=pltpu.CompilerParams(vmem_limit_bytes=MERGE_VMEM),
        name="merge_z",
    )(parts)


def spread_kernel(block_ref, out_ref):
    block = block_ref[...].astype(jnp.float32)
    copies = out_ref.shape[0] // block.shape[0]
    out_ref[...] = jnp.concatenate([block] * copies, axis=0).astype(out_ref.dtype)


def spread(block, copies):
    return pl.pallas_call(
        spread_kernel,
        out_shape=jax.ShapeDtypeStruct((copies * block.shape[0], block.shape[1]), block.dtype),
        compiler_params=pltpu.CompilerParams(vmem_limit_bytes=MERGE_VMEM),
        cost_estimate=pl.CostEstimate(flops=2 * 10**10, bytes_accessed=0, transcendentals=0),
        name="spread",
    )(block)


def project_kernel(context_ref, weight_ref, out_ref):
    blocks, size, _ = out_ref.shape
    product = jnp.dot(context_ref[...], weight_ref[...], preferred_element_type=jnp.float32)
    held = 8
    for b in range(blocks):
        mine = [
            product[(c * blocks + b) * held : (c * blocks + b + 1) * held]
            for c in range(size // held)
        ]
        out_ref[b] = jnp.concatenate(mine, axis=0).astype(jnp.bfloat16)


def project(context, weight, blocks):
    return pl.pallas_call(
        project_kernel,
        out_shape=jax.ShapeDtypeStruct(
            (blocks, context.shape[0] // blocks, weight.shape[1]), jnp.bfloat16
        ),
        compiler_params=pltpu.CompilerParams(vmem_limit_bytes=MERGE_VMEM),
        name="project",
    )(context, weight)


def swap(array, axes):
    return lax.all_to_all(array, axes, split_axis=0, concat_axis=0, tiled=True)


def on_device(
    queries,
    prefix_keys,
    prefix_values,
    suffix_keys,
    suffix_values,
    suffix_lengths,
    slot_request,
    out_weight,
):
    held = queries.shape[0]
    across, along, heads = lax.axis_size("x"), lax.axis_size("z"), lax.axis_size("kvhead")
    near = swap(spread(queries, along), "z")
    def to_other_x(array, turn):
        return lax.ppermute(array, "x", [(i, (i + turn) % across) for i in range(across)])

    turns = range(1, across)
    near = near.reshape(along, held, WIDTH)
    far = [to_other_x(near, turn) for turn in turns]
    first = first_part(near, prefix_keys, prefix_values, across)
    first = suffix_part(
        queries, suffix_keys, suffix_values, suffix_lengths, slot_request, first
    )
    first, *far = lax.optimization_barrier((first, *far))
    leaving = class_part(far, prefix_keys, prefix_values, first, tuple(turns))
    first, *leaving = lax.optimization_barrier((first, *leaving))
    arrived = [to_other_x(part, turn) for part, turn in zip(leaving, turns, strict=True)]
    staying = class_part(far, prefix_keys, prefix_values, first, (0,))
    partial = merge_x([*staying, *arrived])
    context = swap(merge_z(swap(partial, "z"), along, across * along), ("x", "z"))
    out = project(context, out_weight, heads)
    pieces = swap(out.reshape(-1, out.shape[2]), "kvhead")
    pieces = pieces.reshape(heads, across * held, -1).astype(jnp.float32)
    return jnp.sum(pieces, axis=0).astype(jnp.bfloat16)


def solution(mesh):
    x_chips = 4
    devices = mesh.devices
    split = Mesh(
        devices.reshape(x_chips, devices.shape[0] // x_chips, devices.shape[1]),
        ("x", "z", "kvhead"),
    )
    prefix = ("x", "z")
    placed = (
        P(prefix, "kvhead"),
        P(prefix, "kvhead"),
        P(prefix, "kvhead"),
        P(prefix, None, "kvhead"),
        P(prefix, None, "kvhead"),
        P(),
        P(prefix),
        P("kvhead", prefix),
    )
    return jax.shard_map(
        on_device, mesh=split, in_specs=placed, out_specs=P("kvhead", prefix), check_vma=False
    )
```

```python
import functools
import math

import jax
import jax.numpy as jnp
from jax import lax
from jax.experimental import pallas as pl
from jax.experimental.pallas import tpu as pltpu
from jax.sharding import Mesh
from jax.sharding import PartitionSpec as P

HEAD_DIM = 128
GROUP = 8
WIDTH = GROUP * HEAD_DIM
PACKED = WIDTH + HEAD_DIM
SCALE2 = HEAD_DIM ** (-0.5) * math.log2(math.e)
CONTRACT_LAST = (((1,), (1,)), ((), ()))
TURNED = HEAD_DIM + 16
PREFIX_VMEM = 32 << 20
SUFFIX_VMEM = 12 << 20
MERGE_VMEM = 12 << 20


def split3(x):
    high = x.astype(jnp.bfloat16).astype(jnp.float32)
    rest = x - high
    mid = rest.astype(jnp.bfloat16).astype(jnp.float32)
    return high, mid, rest - mid


def operands(k, v):
    return jnp.concatenate([k, k], axis=1), jnp.concatenate([v, jnp.ones_like(v)], axis=1)


def put_queries(rows, base, blocks):
    q = jnp.concatenate([block.astype(jnp.float32) for block in blocks], axis=0) * SCALE2
    slots = q.shape[0]
    for g in range(GROUP):
        here = slice(base + g * slots, base + (g + 1) * slots)
        mine = q[:, g * HEAD_DIM : (g + 1) * HEAD_DIM]
        high = mine.astype(jnp.bfloat16)
        rows[here, :HEAD_DIM] = high
        rows[here, HEAD_DIM:] = (mine - high.astype(jnp.float32)).astype(jnp.bfloat16)


def attend(rows, k_ref, v_ref, acc, peak, step, block):
    total_rows = rows.shape[0]
    for j in range(0, k_ref.shape[0], step):
        k2, v1 = operands(k_ref[j : j + step, :], v_ref[j : j + step, :])
        for r in range(0, total_rows, block):
            scores = lax.dot_general(
                rows[r : r + block, :], k2, CONTRACT_LAST, preferred_element_type=jnp.float32
            )
            probs = jnp.exp2(scores).astype(jnp.bfloat16)
            part = jnp.dot(probs, v1, preferred_element_type=jnp.float32)
            if j == 0:
                acc[r : r + block, :] = part
            else:
                acc[r : r + block, :] += part
    check(rows, k_ref, v_ref, acc, peak)


def attend_turned(rows, k_ref, vt_ref, acc, step):
    turned = 0.0
    for j in range(0, k_ref.shape[0], step):
        k = k_ref[j : j + step, :]
        k2 = jnp.concatenate([k, k], axis=1)
        scores = lax.dot_general(k2, rows[...], CONTRACT_LAST, preferred_element_type=jnp.float32)
        probs = jnp.exp2(scores).astype(jnp.bfloat16)
        turned += jnp.dot(vt_ref[:, j : j + step], probs, preferred_element_type=jnp.float32)
    sums = turned[HEAD_DIM : HEAD_DIM + 1]
    acc[:, :HEAD_DIM] = jnp.transpose(turned[:HEAD_DIM] * (1.0 / sums))
    fine = (sums >= 1e-25) & (sums <= 1e30)
    return jnp.log2(sums), jnp.max(jnp.where(fine, 0.0, 1.0))


def packed_turned(acc, lse, base, slots):
    cut = [slice(base + g * slots, base + (g + 1) * slots) for g in range(GROUP)]
    pieces = [acc[here, :HEAD_DIM].astype(jnp.bfloat16) for here in cut]
    stats = [piece[:, here] for piece in split3(lse) for here in cut]
    stats.append(jnp.zeros((HEAD_DIM - len(stats), slots), jnp.float32))
    stats = jnp.transpose(jnp.concatenate(stats, axis=0))
    return jnp.concatenate(pieces + [stats.astype(jnp.bfloat16)], axis=1)


def check(rows, k_ref, v_ref, acc, peak):
    peak[...] = jnp.zeros_like(peak)
    sums = acc[:, HEAD_DIM:]
    fine = (sums >= 1e-25) & (sums <= 1e30)
    bad = jnp.max(jnp.where(fine, 0.0, 1.0))

    @pl.when(bad > 0.0)
    def _():
        redo(rows, k_ref, v_ref, acc, peak)


def redo(rows, k_ref, v_ref, acc, peak):
    total_rows, length = rows.shape[0], k_ref.shape[0]
    peak[...] = jnp.full_like(peak, -1e38)
    acc[...] = jnp.zeros_like(acc)
    small, few = 512, 128

    def body(i, carry):
        part = pl.ds(pl.multiple_of(i * small, small), small)
        k2, v1 = operands(k_ref[part, :], v_ref[part, :])

        def rows_body(r, inner):
            here = pl.ds(pl.multiple_of(r * few, few), few)
            scores = lax.dot_general(
                rows[here, :], k2, CONTRACT_LAST, preferred_element_type=jnp.float32
            )
            old = peak[here, :]
            new = jnp.maximum(old, jnp.max(scores, axis=1, keepdims=True))
            probs = jnp.exp2(scores - new[:, :1]).astype(jnp.bfloat16)
            decay = jnp.exp2(old[:, :1] - new[:, :1])
            acc[here, :] = acc[here, :] * decay + jnp.dot(
                probs, v1, preferred_element_type=jnp.float32
            )
            peak[here, :] = new
            return inner

        return lax.fori_loop(0, total_rows // few, rows_body, carry)

    lax.fori_loop(0, length // small, body, 0)


def packed(acc, peak, base, slots):
    lane = lax.broadcasted_iota(jnp.int32, (slots, HEAD_DIM), 1)
    stats = jnp.zeros((slots, HEAD_DIM), jnp.float32)
    pieces = []
    for g in range(GROUP):
        here = slice(base + g * slots, base + (g + 1) * slots)
        sums = acc[here, HEAD_DIM:]
        pieces.append((acc[here, :HEAD_DIM] / sums).astype(jnp.bfloat16))
        for n, piece in enumerate(split3(peak[here, :] + jnp.log2(sums))):
            stats = jnp.where(lane == n * GROUP + g, piece, stats)
    return jnp.concatenate(pieces + [stats.astype(jnp.bfloat16)], axis=1)


def first_kernel(q_ref, k_ref, v_ref, out_ref, vt_ref, rows, acc, peak, *, step, block):
    vt_ref[:HEAD_DIM, :] = jnp.transpose(v_ref[...])
    vt_ref[HEAD_DIM:, :] = jnp.ones((TURNED - HEAD_DIM, v_ref.shape[0]), jnp.bfloat16)
    classes = out_ref.shape[0]
    along, held, _ = q_ref.shape
    halves = along // classes
    order = [(c, h) for c in range(classes) for h in range(halves)]
    slots = along * held
    put_queries(rows, 0, [q_ref[h * classes + c] for c, h in order])
    attend(rows, k_ref, v_ref, acc, peak, step, block)
    out = packed(acc, peak, 0, slots)
    size = halves * held
    for c in range(classes):
        out_ref[c] = out[c * size : (c + 1) * size]


def class_kernel(*refs, turns, step):
    *q_refs, k_ref, v_ref, vt_ref, first_ref = refs[: -len(turns) - 3]
    out_refs = refs[-len(turns) - 3 : -3]
    rows, acc, peak = refs[-3:]
    across = first_ref.shape[0]
    along, held, _ = q_refs[0].shape
    halves = along // across
    size = halves * held
    slots = len(q_refs) * size
    here_x = lax.axis_index("x")
    kinds = [lax.rem(here_x + turn, across) for turn in turns]
    for i, kind in enumerate(kinds):
        put_queries(
            rows,
            i * GROUP * slots,
            [q_ref[h * across + kind] for q_ref in q_refs for h in range(halves)],
        )

    def put(outs):
        for out, out_ref, kind in zip(outs, out_refs, kinds, strict=True):
            for n in range(len(q_refs)):
                at = lax.rem(here_x + across - n - 1, across)
                there = pl.ds(pl.multiple_of(at * size, size), size)
                out_ref[there, :] = out[n * size : (n + 1) * size]
            there = pl.ds(pl.multiple_of(here_x * size, size), size)
            out_ref[there, :] = first_ref[kind]

    bases = [i * GROUP * slots for i in range(len(turns))]
    if len(turns) > 1:
        lse, bad = attend_turned(rows, k_ref, vt_ref, acc, step)
        put([packed_turned(acc, lse, base, slots) for base in bases])

        @pl.when(bad > 0.0)
        def _():
            redo(rows, k_ref, v_ref, acc, peak)
            put([packed(acc, peak, base, slots) for base in bases])

    else:
        attend(rows, k_ref, v_ref, acc, peak, 2 * step, rows.shape[0])
        put([packed(acc, peak, base, slots) for base in bases])


def prefix_call(kernel, rows, length, operand_list, out_dims, name):
    vmem = pl.BlockSpec(memory_space=pltpu.VMEM)
    return pl.pallas_call(
        kernel,
        in_specs=[vmem] * len(operand_list),
        out_specs=[vmem] * len(out_dims),
        out_shape=[jax.ShapeDtypeStruct(dims, jnp.bfloat16) for dims in out_dims],
        scratch_shapes=[
            pltpu.VMEM((rows, 2 * HEAD_DIM), jnp.bfloat16),
            pltpu.VMEM((rows, 2 * HEAD_DIM), jnp.float32),
            pltpu.VMEM((rows, HEAD_DIM), jnp.float32),
        ],
        compiler_params=pltpu.CompilerParams(vmem_limit_bytes=PREFIX_VMEM),
        cost_estimate=pl.CostEstimate(
            flops=8 * rows * length * HEAD_DIM,
            bytes_accessed=4 * length * HEAD_DIM,
            transcendentals=rows * length,
        ),
        name=name,
    )(*operand_list)


def first_part(queries, keys, values, classes):
    along, held, _ = queries.shape
    return prefix_call(
        functools.partial(first_kernel, step=4096, block=256),
        GROUP * along * held,
        keys.shape[0],
        (queries, keys, values),
        [(classes, along * held // classes, PACKED), (TURNED, values.shape[0])],
        "first_part",
    )


def class_part(queries, keys, values, turned, first, turns):
    classes, size, _ = first.shape
    rows = GROUP * len(queries) * size
    return prefix_call(
        functools.partial(class_kernel, turns=turns, step=2048),
        rows * len(turns),
        keys.shape[0],
        (*queries, keys, values, turned, first),
        [(classes * size, PACKED)] * len(turns),
        "class_part",
    )


def suffix_kernel(request_ref, lengths_ref, q_ref, keys, values, first_ref, out_ref):
    slots, span = keys.shape[0], keys.shape[1]
    rows = GROUP * slots
    q = jnp.concatenate(
        [q_ref[:, g * HEAD_DIM : (g + 1) * HEAD_DIM].astype(jnp.float32) for g in range(GROUP)],
        axis=0,
    ).astype(jnp.bfloat16)
    slot = lax.rem(lax.broadcasted_iota(jnp.int32, (rows, span), 0), slots)
    limit = jnp.zeros((rows, span), jnp.int32)
    for b in range(slots):
        limit = jnp.where(slot == b, lengths_ref[request_ref[b]], limit)
    live = lax.broadcasted_iota(jnp.int32, (rows, span), 1) < limit
    scores = jnp.zeros((rows, span), jnp.float32)
    for b in range(slots):
        mine = lax.dot_general(q, keys[b], CONTRACT_LAST, preferred_element_type=jnp.float32)
        scores = jnp.where(slot == b, mine, scores)
    scores = jnp.where(live, scores * SCALE2, -1e30)
    top = jnp.max(scores, axis=1, keepdims=True)
    probs = jnp.where(live, jnp.exp2(scores - top), 0.0).astype(jnp.bfloat16).astype(jnp.float32)
    total = jnp.sum(probs, axis=1, keepdims=True)
    numer = jnp.zeros((rows, HEAD_DIM), jnp.float32)
    for b in range(slots):
        mine = jnp.where(slot == b, probs, 0.0).astype(jnp.bfloat16)
        numer += jnp.dot(mine, values[b], preferred_element_type=jnp.float32)
    ctx = numer / total
    lse = jnp.broadcast_to(top + jnp.log2(total), (rows, HEAD_DIM))
    classes, size, _ = first_ref.shape
    here_z = lax.axis_index("z")
    kind, half = lax.rem(here_z, classes), here_z // classes
    own = lax.broadcasted_iota(jnp.int32, (size, WIDTH), 0) // slots == half

    def across_lanes(array):
        array = jnp.concatenate([array[g * slots : (g + 1) * slots] for g in range(GROUP)], axis=1)
        return jnp.concatenate([array] * (size // slots), axis=0)

    prefix = first_ref[kind]
    prefix_ctx = prefix[:, :WIDTH].astype(jnp.float32)
    prefix_lse = spread_lse(prefix[:, WIDTH:])
    both_ctx, both_lse = weighted([prefix_ctx, across_lanes(ctx)], [prefix_lse, across_lanes(lse)])
    out_ref[...] = first_ref[...]
    out_ref[kind, :, :WIDTH] = jnp.where(own, both_ctx, prefix_ctx).astype(jnp.bfloat16)
    out_ref[kind, :, WIDTH:] = pack_lse(jnp.where(own, both_lse, prefix_lse))


def suffix_part(queries, keys, values, lengths, request, first):
    vmem = pl.BlockSpec(memory_space=pltpu.VMEM)
    smem = pl.BlockSpec(memory_space=pltpu.SMEM)
    return pl.pallas_call(
        suffix_kernel,
        in_specs=[smem, smem, vmem, vmem, vmem, vmem],
        out_specs=vmem,
        out_shape=jax.ShapeDtypeStruct(first.shape, jnp.bfloat16),
        compiler_params=pltpu.CompilerParams(vmem_limit_bytes=SUFFIX_VMEM),
        name="suffix_part",
    )(request, lengths, queries, keys, values, first)


def spread_lse(stats):
    source = lax.broadcasted_iota(jnp.int32, (HEAD_DIM, WIDTH), 0)
    head = lax.broadcasted_iota(jnp.int32, (HEAD_DIM, WIDTH), 1) // HEAD_DIM
    chosen = (lax.rem(source, GROUP) == head) & (source < 3 * GROUP)
    chosen = jnp.where(chosen, 1.0, 0.0).astype(jnp.bfloat16)
    return jnp.dot(stats, chosen, preferred_element_type=jnp.float32)


def weighted(parts, lse):
    top = functools.reduce(jnp.maximum, lse)
    total, numer = 0.0, 0.0
    for part, each in zip(parts, lse, strict=True):
        weight = jnp.exp2(each - top)
        total += weight
        numer += weight * part
    return numer / total, top + jnp.log2(total)


def pack_lse(lse):
    rows = lse.shape[0]
    lane = lax.broadcasted_iota(jnp.int32, (rows, HEAD_DIM), 1)
    stats = jnp.zeros((rows, HEAD_DIM), jnp.float32)
    for g in range(GROUP):
        for n, piece in enumerate(split3(lse[:, g * HEAD_DIM : (g + 1) * HEAD_DIM])):
            stats = jnp.where(lane == n * GROUP + g, piece, stats)
    return stats.astype(jnp.bfloat16)


def merge_x_kernel(*refs):
    *part_refs, out_ref = refs
    ctx, both = weighted(
        [part[:, :WIDTH].astype(jnp.float32) for part in part_refs],
        [spread_lse(part[:, WIDTH:]) for part in part_refs],
    )
    out_ref[:, :WIDTH] = ctx.astype(jnp.bfloat16)
    out_ref[:, WIDTH:] = pack_lse(both)


def merge_x(parts):
    return pl.pallas_call(
        merge_x_kernel,
        out_shape=jax.ShapeDtypeStruct(parts[0].shape, jnp.bfloat16),
        compiler_params=pltpu.CompilerParams(vmem_limit_bytes=MERGE_VMEM),
        name="merge_x",
    )(*parts)


def merge_z_kernel(parts_ref, out_ref, *, sources):
    slots = parts_ref.shape[0] // sources
    lse = spread_lse(parts_ref[:, WIDTH:])
    parts = parts_ref[:, :WIDTH].astype(jnp.float32)
    cut = [slice(i * slots, (i + 1) * slots) for i in range(sources)]
    context, _ = weighted([parts[c] for c in cut], [lse[c] for c in cut])
    out_ref[...] = jnp.concatenate([context] * (out_ref.shape[0] // slots), axis=0).astype(jnp.bfloat16)


def merge_z(parts, sources, copies):
    return pl.pallas_call(
        functools.partial(merge_z_kernel, sources=sources),
        out_shape=jax.ShapeDtypeStruct((parts.shape[0] // sources * copies, WIDTH), jnp.bfloat16),
        compiler_params=pltpu.CompilerParams(vmem_limit_bytes=MERGE_VMEM),
        name="merge_z",
    )(parts)


def spread_kernel(block_ref, out_ref):
    block = block_ref[...].astype(jnp.float32)
    copies = out_ref.shape[0] // block.shape[0]
    out_ref[...] = jnp.concatenate([block] * copies, axis=0).astype(out_ref.dtype)


def spread(block, copies):
    return pl.pallas_call(
        spread_kernel,
        out_shape=jax.ShapeDtypeStruct((copies * block.shape[0], block.shape[1]), block.dtype),
        compiler_params=pltpu.CompilerParams(vmem_limit_bytes=MERGE_VMEM),
        cost_estimate=pl.CostEstimate(flops=2 * 10**10, bytes_accessed=0, transcendentals=0),
        name="spread",
    )(block)


def project_kernel(context_ref, weight_ref, out_ref):
    blocks, size, _ = out_ref.shape
    product = jnp.dot(context_ref[...], weight_ref[...], preferred_element_type=jnp.float32)
    held = 8
    for b in range(blocks):
        mine = [
            product[(c * blocks + b) * held : (c * blocks + b + 1) * held]
            for c in range(size // held)
        ]
        out_ref[b] = jnp.concatenate(mine, axis=0).astype(jnp.bfloat16)


def project(context, weight, blocks):
    return pl.pallas_call(
        project_kernel,
        out_shape=jax.ShapeDtypeStruct(
            (blocks, context.shape[0] // blocks, weight.shape[1]), jnp.bfloat16
        ),
        compiler_params=pltpu.CompilerParams(vmem_limit_bytes=MERGE_VMEM),
        name="project",
    )(context, weight)


def swap(array, axes):
    return lax.all_to_all(array, axes, split_axis=0, concat_axis=0, tiled=True)


def on_device(
    queries,
    prefix_keys,
    prefix_values,
    suffix_keys,
    suffix_values,
    suffix_lengths,
    slot_request,
    out_weight,
):
    held = queries.shape[0]
    across, along, heads = lax.axis_size("x"), lax.axis_size("z"), lax.axis_size("kvhead")
    near = swap(spread(queries, along), "z")
    def to_other_x(array, turn):
        return lax.ppermute(array, "x", [(i, (i + turn) % across) for i in range(across)])

    turns = range(1, across)
    near = near.reshape(along, held, WIDTH)
    far = [to_other_x(near, turn) for turn in turns]
    first, turned = first_part(near, prefix_keys, prefix_values, across)
    first = suffix_part(
        queries, suffix_keys, suffix_values, suffix_lengths, slot_request, first
    )
    first, *far = lax.optimization_barrier((first, *far))
    leaving = class_part(far, prefix_keys, prefix_values, turned, first, tuple(turns))
    first, *leaving = lax.optimization_barrier((first, *leaving))
    arrived = [to_other_x(part, turn) for part, turn in zip(leaving, turns, strict=True)]
    staying = class_part(far, prefix_keys, prefix_values, turned, first, (0,))
    partial = merge_x([*staying, *arrived])
    context = swap(merge_z(swap(partial, "z"), along, across * along), ("x", "z"))
    out = project(context, out_weight, heads)
    pieces = swap(out.reshape(-1, out.shape[2]), "kvhead")
    pieces = pieces.reshape(heads, across * held, -1).astype(jnp.float32)
    return jnp.sum(pieces, axis=0).astype(jnp.bfloat16)


def solution(mesh):
    x_chips = 4
    devices = mesh.devices
    split = Mesh(
        devices.reshape(x_chips, devices.shape[0] // x_chips, devices.shape[1]),
        ("x", "z", "kvhead"),
    )
    prefix = ("x", "z")
    placed = (
        P(prefix, "kvhead"),
        P(prefix, "kvhead"),
        P(prefix, "kvhead"),
        P(prefix, None, "kvhead"),
        P(prefix, None, "kvhead"),
        P(),
        P(prefix),
        P("kvhead", prefix),
    )
    return jax.shard_map(
        on_device, mesh=split, in_specs=placed, out_specs=P("kvhead", prefix), check_vma=False
    )
```

```python
import functools
import math

import jax
import jax.numpy as jnp
from jax import lax
from jax.experimental import pallas as pl
from jax.experimental.pallas import tpu as pltpu
from jax.sharding import Mesh
from jax.sharding import PartitionSpec as P

HEAD_DIM = 128
GROUP = 8
WIDTH = GROUP * HEAD_DIM
PACKED = WIDTH + HEAD_DIM
SCALE2 = HEAD_DIM ** (-0.5) * math.log2(math.e)
CONTRACT_LAST = (((1,), (1,)), ((), ()))
TURNED = HEAD_DIM + 16
PREFIX_VMEM = 32 << 20
SUFFIX_VMEM = 12 << 20
MERGE_VMEM = 12 << 20


def split3(x):
    high = x.astype(jnp.bfloat16).astype(jnp.float32)
    rest = x - high
    mid = rest.astype(jnp.bfloat16).astype(jnp.float32)
    return high, mid, rest - mid


def operands(k, v):
    return jnp.concatenate([k, k], axis=1), jnp.concatenate([v, jnp.ones_like(v)], axis=1)


def put_queries(rows, base, blocks):
    q = jnp.concatenate([block.astype(jnp.float32) for block in blocks], axis=0) * SCALE2
    slots = q.shape[0]
    for g in range(GROUP):
        here = slice(base + g * slots, base + (g + 1) * slots)
        mine = q[:, g * HEAD_DIM : (g + 1) * HEAD_DIM]
        high = mine.astype(jnp.bfloat16)
        rows[here, :HEAD_DIM] = high
        rows[here, HEAD_DIM:] = (mine - high.astype(jnp.float32)).astype(jnp.bfloat16)


def attend(rows, k_ref, v_ref, acc, peak, step, block):
    total_rows = rows.shape[0]
    for j in range(0, k_ref.shape[0], step):
        k2, v1 = operands(k_ref[j : j + step, :], v_ref[j : j + step, :])
        for r in range(0, total_rows, block):
            scores = lax.dot_general(
                rows[r : r + block, :], k2, CONTRACT_LAST, preferred_element_type=jnp.float32
            )
            probs = jnp.exp2(scores).astype(jnp.bfloat16)
            part = jnp.dot(probs, v1, preferred_element_type=jnp.float32)
            if j == 0:
                acc[r : r + block, :] = part
            else:
                acc[r : r + block, :] += part
    check(rows, k_ref, v_ref, acc, peak)


def attend_turned(rows, k_ref, vt_ref, acc, step):
    turned = 0.0
    for j in range(0, k_ref.shape[0], step):
        k = k_ref[j : j + step, :]
        k2 = jnp.concatenate([k, k], axis=1)
        scores = lax.dot_general(k2, rows[...], CONTRACT_LAST, preferred_element_type=jnp.float32)
        probs = jnp.exp2(scores).astype(jnp.bfloat16)
        turned += jnp.dot(vt_ref[:, j : j + step], probs, preferred_element_type=jnp.float32)
    sums = turned[HEAD_DIM : HEAD_DIM + 1]
    acc[:, :HEAD_DIM] = jnp.transpose(turned[:HEAD_DIM] * (1.0 / sums))
    fine = (sums >= 1e-25) & (sums <= 1e30)
    return jnp.log2(sums), jnp.max(jnp.where(fine, 0.0, 1.0))


def packed_turned(acc, lse, base, slots):
    cut = [slice(base + g * slots, base + (g + 1) * slots) for g in range(GROUP)]
    pieces = [acc[here, :HEAD_DIM].astype(jnp.bfloat16) for here in cut]
    stats = [piece[:, here] for piece in split3(lse) for here in cut]
    stats.append(jnp.zeros((HEAD_DIM - len(stats), slots), jnp.float32))
    stats = jnp.transpose(jnp.concatenate(stats, axis=0))
    return jnp.concatenate(pieces + [stats.astype(jnp.bfloat16)], axis=1)


def check(rows, k_ref, v_ref, acc, peak):
    peak[...] = jnp.zeros_like(peak)
    sums = acc[:, HEAD_DIM:]
    fine = (sums >= 1e-25) & (sums <= 1e30)
    bad = jnp.max(jnp.where(fine, 0.0, 1.0))

    @pl.when(bad > 0.0)
    def _():
        redo(rows, k_ref, v_ref, acc, peak)


def redo(rows, k_ref, v_ref, acc, peak):
    total_rows, length = rows.shape[0], k_ref.shape[0]
    peak[...] = jnp.full_like(peak, -1e38)
    acc[...] = jnp.zeros_like(acc)
    small, few = 512, 128

    def body(i, carry):
        part = pl.ds(pl.multiple_of(i * small, small), small)
        k2, v1 = operands(k_ref[part, :], v_ref[part, :])

        def rows_body(r, inner):
            here = pl.ds(pl.multiple_of(r * few, few), few)
            scores = lax.dot_general(
                rows[here, :], k2, CONTRACT_LAST, preferred_element_type=jnp.float32
            )
            old = peak[here, :]
            new = jnp.maximum(old, jnp.max(scores, axis=1, keepdims=True))
            probs = jnp.exp2(scores - new[:, :1]).astype(jnp.bfloat16)
            decay = jnp.exp2(old[:, :1] - new[:, :1])
            acc[here, :] = acc[here, :] * decay + jnp.dot(
                probs, v1, preferred_element_type=jnp.float32
            )
            peak[here, :] = new
            return inner

        return lax.fori_loop(0, total_rows // few, rows_body, carry)

    lax.fori_loop(0, length // small, body, 0)


def packed(acc, peak, base, slots):
    lane = lax.broadcasted_iota(jnp.int32, (slots, HEAD_DIM), 1)
    stats = jnp.zeros((slots, HEAD_DIM), jnp.float32)
    pieces = []
    for g in range(GROUP):
        here = slice(base + g * slots, base + (g + 1) * slots)
        sums = acc[here, HEAD_DIM:]
        pieces.append((acc[here, :HEAD_DIM] / sums).astype(jnp.bfloat16))
        for n, piece in enumerate(split3(peak[here, :] + jnp.log2(sums))):
            stats = jnp.where(lane == n * GROUP + g, piece, stats)
    return jnp.concatenate(pieces + [stats.astype(jnp.bfloat16)], axis=1)


def first_kernel(q_ref, k_ref, v_ref, out_ref, vt_ref, rows, acc, peak, *, step, block):
    vt_ref[:HEAD_DIM, :] = jnp.transpose(v_ref[...])
    vt_ref[HEAD_DIM:, :] = jnp.ones((TURNED - HEAD_DIM, v_ref.shape[0]), jnp.bfloat16)
    classes = out_ref.shape[0]
    along, held, _ = q_ref.shape
    halves = along // classes
    order = [(c, h) for c in range(classes) for h in range(halves)]
    slots = along * held
    put_queries(rows, 0, [q_ref[h * classes + c] for c, h in order])
    attend(rows, k_ref, v_ref, acc, peak, step, block)
    out = packed(acc, peak, 0, slots)
    size = halves * held
    for c in range(classes):
        out_ref[c] = out[c * size : (c + 1) * size]


def class_kernel(*refs, turns, step):
    *q_refs, k_ref, v_ref, vt_ref, first_ref = refs[: -len(turns) - 3]
    out_refs = refs[-len(turns) - 3 : -3]
    rows, acc, peak = refs[-3:]
    across = first_ref.shape[0]
    along, held, _ = q_refs[0].shape
    halves = along // across
    size = halves * held
    slots = len(q_refs) * size
    here_x = lax.axis_index("x")
    kinds = [lax.bitwise_xor(here_x, jnp.int32(turn)) for turn in turns]
    for i, kind in enumerate(kinds):
        put_queries(
            rows,
            i * GROUP * slots,
            [q_ref[h * across + kind] for q_ref in q_refs for h in range(halves)],
        )

    def put(outs):
        for out, out_ref, kind in zip(outs, out_refs, kinds, strict=True):
            for n in range(len(q_refs)):
                at = lax.bitwise_xor(here_x, jnp.int32(n + 1))
                there = pl.ds(pl.multiple_of(at * size, size), size)
                out_ref[there, :] = out[n * size : (n + 1) * size]
            there = pl.ds(pl.multiple_of(here_x * size, size), size)
            out_ref[there, :] = first_ref[kind]

    bases = [i * GROUP * slots for i in range(len(turns))]
    if len(turns) > 1:
        lse, bad = attend_turned(rows, k_ref, vt_ref, acc, step)
        put([packed_turned(acc, lse, base, slots) for base in bases])

        @pl.when(bad > 0.0)
        def _():
            redo(rows, k_ref, v_ref, acc, peak)
            put([packed(acc, peak, base, slots) for base in bases])

    else:
        attend(rows, k_ref, v_ref, acc, peak, 2 * step, rows.shape[0])
        put([packed(acc, peak, base, slots) for base in bases])


def prefix_call(kernel, rows, length, operand_list, out_dims, name):
    vmem = pl.BlockSpec(memory_space=pltpu.VMEM)
    return pl.pallas_call(
        kernel,
        in_specs=[vmem] * len(operand_list),
        out_specs=[vmem] * len(out_dims),
        out_shape=[jax.ShapeDtypeStruct(dims, jnp.bfloat16) for dims in out_dims],
        scratch_shapes=[
            pltpu.VMEM((rows, 2 * HEAD_DIM), jnp.bfloat16),
            pltpu.VMEM((rows, 2 * HEAD_DIM), jnp.float32),
            pltpu.VMEM((rows, HEAD_DIM), jnp.float32),
        ],
        compiler_params=pltpu.CompilerParams(vmem_limit_bytes=PREFIX_VMEM),
        cost_estimate=pl.CostEstimate(
            flops=8 * rows * length * HEAD_DIM,
            bytes_accessed=4 * length * HEAD_DIM,
            transcendentals=rows * length,
        ),
        name=name,
    )(*operand_list)


def first_part(queries, keys, values, classes):
    along, held, _ = queries.shape
    return prefix_call(
        functools.partial(first_kernel, step=4096, block=256),
        GROUP * along * held,
        keys.shape[0],
        (queries, keys, values),
        [(classes, along * held // classes, PACKED), (TURNED, values.shape[0])],
        "first_part",
    )


def class_part(queries, keys, values, turned, first, turns):
    classes, size, _ = first.shape
    rows = GROUP * len(queries) * size
    return prefix_call(
        functools.partial(class_kernel, turns=turns, step=2048),
        rows * len(turns),
        keys.shape[0],
        (*queries, keys, values, turned, first),
        [(classes * size, PACKED)] * len(turns),
        "class_part",
    )


def suffix_kernel(request_ref, lengths_ref, q_ref, keys, values, first_ref, out_ref):
    slots, span = keys.shape[0], keys.shape[1]
    rows = GROUP * slots
    q = jnp.concatenate(
        [q_ref[:, g * HEAD_DIM : (g + 1) * HEAD_DIM].astype(jnp.float32) for g in range(GROUP)],
        axis=0,
    ).astype(jnp.bfloat16)
    slot = lax.rem(lax.broadcasted_iota(jnp.int32, (rows, span), 0), slots)
    limit = jnp.zeros((rows, span), jnp.int32)
    for b in range(slots):
        limit = jnp.where(slot == b, lengths_ref[request_ref[b]], limit)
    live = lax.broadcasted_iota(jnp.int32, (rows, span), 1) < limit
    scores = jnp.zeros((rows, span), jnp.float32)
    for b in range(slots):
        mine = lax.dot_general(q, keys[b], CONTRACT_LAST, preferred_element_type=jnp.float32)
        scores = jnp.where(slot == b, mine, scores)
    scores = jnp.where(live, scores * SCALE2, -1e30)
    top = jnp.max(scores, axis=1, keepdims=True)
    probs = jnp.where(live, jnp.exp2(scores - top), 0.0).astype(jnp.bfloat16).astype(jnp.float32)
    total = jnp.sum(probs, axis=1, keepdims=True)
    numer = jnp.zeros((rows, HEAD_DIM), jnp.float32)
    for b in range(slots):
        mine = jnp.where(slot == b, probs, 0.0).astype(jnp.bfloat16)
        numer += jnp.dot(mine, values[b], preferred_element_type=jnp.float32)
    ctx = numer / total
    lse = jnp.broadcast_to(top + jnp.log2(total), (rows, HEAD_DIM))
    classes, size, _ = first_ref.shape
    here_z = lax.axis_index("z")
    kind, half = lax.rem(here_z, classes), here_z // classes
    own = lax.broadcasted_iota(jnp.int32, (size, WIDTH), 0) // slots == half

    def across_lanes(array):
        array = jnp.concatenate([array[g * slots : (g + 1) * slots] for g in range(GROUP)], axis=1)
        return jnp.concatenate([array] * (size // slots), axis=0)

    prefix = first_ref[kind]
    prefix_ctx = prefix[:, :WIDTH].astype(jnp.float32)
    prefix_lse = spread_lse(prefix[:, WIDTH:])
    both_ctx, both_lse = weighted([prefix_ctx, across_lanes(ctx)], [prefix_lse, across_lanes(lse)])
    out_ref[...] = first_ref[...]
    out_ref[kind, :, :WIDTH] = jnp.where(own, both_ctx, prefix_ctx).astype(jnp.bfloat16)
    out_ref[kind, :, WIDTH:] = pack_lse(jnp.where(own, both_lse, prefix_lse))


def suffix_part(queries, keys, values, lengths, request, first):
    vmem = pl.BlockSpec(memory_space=pltpu.VMEM)
    smem = pl.BlockSpec(memory_space=pltpu.SMEM)
    return pl.pallas_call(
        suffix_kernel,
        in_specs=[smem, smem, vmem, vmem, vmem, vmem],
        out_specs=vmem,
        out_shape=jax.ShapeDtypeStruct(first.shape, jnp.bfloat16),
        compiler_params=pltpu.CompilerParams(vmem_limit_bytes=SUFFIX_VMEM),
        name="suffix_part",
    )(request, lengths, queries, keys, values, first)


def spread_lse(stats):
    source = lax.broadcasted_iota(jnp.int32, (HEAD_DIM, WIDTH), 0)
    head = lax.broadcasted_iota(jnp.int32, (HEAD_DIM, WIDTH), 1) // HEAD_DIM
    chosen = (lax.rem(source, GROUP) == head) & (source < 3 * GROUP)
    chosen = jnp.where(chosen, 1.0, 0.0).astype(jnp.bfloat16)
    return jnp.dot(stats, chosen, preferred_element_type=jnp.float32)


def weighted(parts, lse):
    top = functools.reduce(jnp.maximum, lse)
    total, numer = 0.0, 0.0
    for part, each in zip(parts, lse, strict=True):
        weight = jnp.exp2(each - top)
        total += weight
        numer += weight * part
    return numer / total, top + jnp.log2(total)


def pack_lse(lse):
    rows = lse.shape[0]
    lane = lax.broadcasted_iota(jnp.int32, (rows, HEAD_DIM), 1)
    stats = jnp.zeros((rows, HEAD_DIM), jnp.float32)
    for g in range(GROUP):
        for n, piece in enumerate(split3(lse[:, g * HEAD_DIM : (g + 1) * HEAD_DIM])):
            stats = jnp.where(lane == n * GROUP + g, piece, stats)
    return stats.astype(jnp.bfloat16)


def merge_x_kernel(*refs):
    *part_refs, out_ref = refs
    ctx, both = weighted(
        [part[:, :WIDTH].astype(jnp.float32) for part in part_refs],
        [spread_lse(part[:, WIDTH:]) for part in part_refs],
    )
    out_ref[:, :WIDTH] = ctx.astype(jnp.bfloat16)
    out_ref[:, WIDTH:] = pack_lse(both)


def merge_x(parts):
    return pl.pallas_call(
        merge_x_kernel,
        out_shape=jax.ShapeDtypeStruct(parts[0].shape, jnp.bfloat16),
        compiler_params=pltpu.CompilerParams(vmem_limit_bytes=MERGE_VMEM),
        name="merge_x",
    )(*parts)


def merge_z_kernel(parts_ref, out_ref, *, sources):
    slots = parts_ref.shape[0] // sources
    lse = spread_lse(parts_ref[:, WIDTH:])
    parts = parts_ref[:, :WIDTH].astype(jnp.float32)
    cut = [slice(i * slots, (i + 1) * slots) for i in range(sources)]
    context, _ = weighted([parts[c] for c in cut], [lse[c] for c in cut])
    out_ref[...] = jnp.concatenate([context] * (out_ref.shape[0] // slots), axis=0).astype(jnp.bfloat16)


def merge_z(parts, sources, copies):
    return pl.pallas_call(
        functools.partial(merge_z_kernel, sources=sources),
        out_shape=jax.ShapeDtypeStruct((parts.shape[0] // sources * copies, WIDTH), jnp.bfloat16),
        compiler_params=pltpu.CompilerParams(vmem_limit_bytes=MERGE_VMEM),
        name="merge_z",
    )(parts)


def spread_kernel(block_ref, out_ref):
    block = block_ref[...].astype(jnp.float32)
    copies = out_ref.shape[0] // block.shape[0]
    out_ref[...] = jnp.concatenate([block] * copies, axis=0).astype(out_ref.dtype)


def spread(block, copies):
    return pl.pallas_call(
        spread_kernel,
        out_shape=jax.ShapeDtypeStruct((copies * block.shape[0], block.shape[1]), block.dtype),
        compiler_params=pltpu.CompilerParams(vmem_limit_bytes=MERGE_VMEM),
        cost_estimate=pl.CostEstimate(flops=2 * 10**10, bytes_accessed=0, transcendentals=0),
        name="spread",
    )(block)


def project_kernel(context_ref, weight_ref, out_ref):
    blocks, size, _ = out_ref.shape
    product = jnp.dot(context_ref[...], weight_ref[...], preferred_element_type=jnp.float32)
    held = 8
    for b in range(blocks):
        mine = [
            product[(c * blocks + b) * held : (c * blocks + b + 1) * held]
            for c in range(size // held)
        ]
        out_ref[b] = jnp.concatenate(mine, axis=0).astype(jnp.bfloat16)


def project(context, weight, blocks):
    return pl.pallas_call(
        project_kernel,
        out_shape=jax.ShapeDtypeStruct(
            (blocks, context.shape[0] // blocks, weight.shape[1]), jnp.bfloat16
        ),
        compiler_params=pltpu.CompilerParams(vmem_limit_bytes=MERGE_VMEM),
        name="project",
    )(context, weight)


def swap(array, axes):
    return lax.all_to_all(array, axes, split_axis=0, concat_axis=0, tiled=True)


def on_device(
    queries,
    prefix_keys,
    prefix_values,
    suffix_keys,
    suffix_values,
    suffix_lengths,
    slot_request,
    out_weight,
):
    held = queries.shape[0]
    across, along, heads = lax.axis_size("x"), lax.axis_size("z"), lax.axis_size("kvhead")
    near = swap(spread(queries, along), "z")
    def to_other_x(array, turn):
        return lax.ppermute(array, "x", [(i, i ^ turn) for i in range(across)])

    turns = range(1, across)
    near = near.reshape(along, held, WIDTH)
    far = [to_other_x(near, turn) for turn in turns]
    first, turned = first_part(near, prefix_keys, prefix_values, across)
    first = suffix_part(
        queries, suffix_keys, suffix_values, suffix_lengths, slot_request, first
    )
    first, *far = lax.optimization_barrier((first, *far))
    leaving = class_part(far, prefix_keys, prefix_values, turned, first, tuple(turns))
    first, *leaving = lax.optimization_barrier((first, *leaving))
    arrived = [to_other_x(part, turn) for part, turn in zip(leaving, turns, strict=True)]
    staying = class_part(far, prefix_keys, prefix_values, turned, first, (0,))
    partial = merge_x([*staying, *arrived])
    context = swap(merge_z(swap(partial, "z"), along, across * along), ("x", "z"))
    out = project(context, out_weight, heads)
    pieces = swap(out.reshape(-1, out.shape[2]), "kvhead")
    pieces = pieces.reshape(heads, across * held, -1).astype(jnp.float32)
    return jnp.sum(pieces, axis=0).astype(jnp.bfloat16)


def solution(mesh):
    x_chips = 4
    devices = mesh.devices
    split = Mesh(
        devices.reshape(x_chips, devices.shape[0] // x_chips, devices.shape[1]),
        ("x", "z", "kvhead"),
    )
    prefix = ("x", "z")
    placed = (
        P(prefix, "kvhead"),
        P(prefix, "kvhead"),
        P(prefix, "kvhead"),
        P(prefix, None, "kvhead"),
        P(prefix, None, "kvhead"),
        P(),
        P(prefix),
        P("kvhead", prefix),
    )
    return jax.shard_map(
        on_device, mesh=split, in_specs=placed, out_specs=P("kvhead", prefix), check_vma=False
    )
```
